32 devices in a mesh: sky: 16 (over z, y, core), epoch: 2 (over x).
Axes of the slice: x: 2, y: 2, z: 4, core: 2. Of those that a mesh axis runs over, the one named last changes fastest.
Arguments:
- visits: float32 [2, 2048, 1024], P('epoch', 'sky'), may hold values from -6 to 6
- template: float32 [2048, 1024], P(('sky', 'epoch')), may hold values from -6 to 6
- basis_taps: float32 [2, 27, 17], replicated, may hold values from -1.5 to 1.5
- coeffs: float32 [2, 16, 27, 3], P('epoch', 'sky'), may hold values from -1.2 to 1.2
- psf_taps: float32 [2, 9], P('epoch'), may hold values from -2 to 2
- inv_var: float32 [2, 2048, 1024], P('epoch', 'sky'), may hold values from 0.3 to 3
- shifts: int32 [16, 24, 2, 2], P('sky'), may hold values from -16 to 16
- vel_count: int32 [16], P('sky'), may hold values from 1 to 24, 192 in all
Outputs:
- best_map: float32 [2048, 1024], P(('sky', 'epoch'))
The draws below stay inside these ranges and needn't reach their ends.
Inputs may be any that keep to these rules, and one draw needn't show every extreme that they name: `shifts`: a velocity's shift of one epoch, row first, in whole pixels. Velocities 0 to vel_count - 1 of a tile are searched; some tile searches all 24.
All inputs are finite; a program needn't handle non-finite values. No bound on the sum of `vel_count` on one device may be relied on, other than what follows from the above.
Results may differ from the reference program's by a relative error of at most 0.0026.
Values may be sent and summed in bfloat16 or wider, within the bound.
A program may use at most 128 MiB of HBM per device.

```python
import math
import jax
import jax.numpy as jnp
import numpy as np
from jax import lax

H = 128
W = 1024
NB = 27
R = 8
F = 4
SMAX = 16
NV = 24
EPOCHS = 2
TILES = 16


def set_ends(values, stream_key, least, largest):
    longest = values.shape.index(max(values.shape))
    spots = []
    for shift in (0, 1):
        where = [jax.random.randint(jax.random.fold_in(stream_key, axis), (), 0, length) for axis, length in enumerate(values.shape)]
        where[longest] = (where[longest] + shift) % values.shape[longest]
        spots.append(tuple(where))
    return values.at[spots[0]].set(least).at[spots[1]].set(largest)


def block_scale(rng, extent, pieces, smallest, top_value):
    loudness = 1.0
    for axis_at, blocks in pieces:
        heights = jax.random.uniform(jax.random.fold_in(jax.random.fold_in(rng, 6), axis_at), (blocks,), jnp.float32, smallest / len(pieces), top_value / len(pieces))
        loudness = loudness * jnp.repeat(jnp.exp(heights), extent[axis_at] // blocks).reshape((-1,) + (1,) * (len(extent) - 1 - axis_at))
    return loudness


def length_profile(count, total, bound, lean):
    weights = [(1 << 20) // math.isqrt(rank ** lean) + 1 for rank in range(2, count + 1)]
    spare, counts = total - bound - (count - 1), [1] * (count - 1)
    while spare > 0:
        movable = [i for i in range(count - 1) if counts[i] < bound]
        pool, remaining = sum([weights[i] for i in movable]), spare
        for i in movable:
            more = min(bound - counts[i], max(1, remaining * weights[i] // pool), spare)
            counts[i] = counts[i] + more
            spare = spare - more
    return np.array([bound] + counts)


def ragged(own_key, amount, total, bound, lean):
    if amount == 2:
        one = jax.random.randint(own_key, (), max(1, total - bound), min(bound, total - 1) + 1)
        return jnp.stack([one, total - one])
    sizes = jnp.asarray(length_profile(amount, total, bound, lean), jnp.int32)
    twos = (amount - 1) // 2
    source_of, sink = sizes[1:1 + 2 * twos:2], sizes[2:2 + 2 * twos:2]
    slack = jnp.minimum(source_of - 1, bound - sink)
    moved = jax.random.randint(jax.random.fold_in(own_key, 1), (twos,), 0, 1 << 20) % (slack + 1)
    sizes = sizes.at[1:1 + 2 * twos:2].set(source_of - moved).at[2:2 + 2 * twos:2].set(sink + moved)
    return sizes[jax.random.permutation(jax.random.fold_in(own_key, 2), amount)]


def bell_draw(key, extent, width, limit, pieces=(), kind=jnp.bfloat16):
    gain = block_scale(key, extent, pieces, -0.22, 0.18) if pieces else 1.0
    entries = jax.random.normal(key, extent, jnp.float32) * width * gain
    return jnp.minimum(jnp.maximum(entries, -limit), limit).astype(kind)


def setup_inputs(seed: int = 0) -> dict:
    key_of = jax.random.split(jax.random.key(seed), 9)
    visits = bell_draw(key_of[0], (EPOCHS, TILES * H, W), 1.0, 6.0, ((0, 2), (1, 16)), jnp.float32)
    template = bell_draw(key_of[1], (TILES * H, W), 1.0, 6.0, ((0, 32),), jnp.float32)
    basis_taps = bell_draw(key_of[2], (2, NB, 2 * R + 1), (2 * R + 1) ** -0.5, 1.5, (), jnp.float32)
    coeffs = bell_draw(key_of[3], (EPOCHS, TILES, NB, 3), 0.2, 1.2, ((0, 2), (1, 16)), jnp.float32)
    psf_taps = bell_draw(key_of[4], (EPOCHS, 2 * F + 1), (2 * F + 1) ** -0.5, 2.0, ((0, 2),), jnp.float32)
    inv_var = jnp.clip(jnp.exp(math.log(3.0) - 2.3025851 * jax.random.uniform(key_of[5], (EPOCHS, TILES * H, W), jnp.float32) ** block_scale(key_of[5], (EPOCHS, TILES * H, W), ((0, 2), (1, 16)), -0.2, 0.2)), 0.3, 3.0)
    shifts = set_ends(jax.random.randint(key_of[6], (TILES, NV, EPOCHS, 2), 0 - SMAX, SMAX + 1), jax.random.fold_in(key_of[6], 1), 0 - SMAX, SMAX).astype(jnp.int32)
    vel_count = ragged(key_of[7], TILES, TILES * NV // 2, NV, 2).astype(jnp.int32)
    return dict(visits=visits, template=template, basis_taps=basis_taps, coeffs=coeffs, psf_taps=psf_taps, inv_var=inv_var, shifts=shifts, vel_count=vel_count)


def conv_rows(extended, kernel, half_width):
    height = extended.shape[0] - 2 * half_width
    result = kernel[0] * extended[0:height]
    for offset in range(1, 2 * half_width + 1):
        result = result + kernel[offset] * extended[offset:offset + height]
    return result

def conv_cols(image, kernel, half_width):
    columns = image.shape[1]
    padded = jnp.pad(image, ((0, 0), (half_width, half_width)))
    result = kernel[0] * padded[:, 0:columns]
    for offset in range(1, 2 * half_width + 1):
        result = result + kernel[offset] * padded[:, offset:offset + columns]
    return result

def normalized(position, length):
    return (position - (length - 1) / 2.0) / ((length - 1) / 2.0)

def reference(visits, template, basis_taps, coeffs, psf_taps, inv_var, shifts, vel_count):
    rows = template.shape[0]
    columns = template.shape[1]
    extended = jnp.pad(template, ((R, R), (0, 0)))
    basis_maps = [conv_cols(conv_rows(extended, basis_taps[0, basis_index], R), basis_taps[1, basis_index], R) for basis_index in range(NB)]
    row_pos = normalized((jnp.arange(rows, dtype=jnp.int32) % H).astype(jnp.float32), H)[:, None]
    col_pos = normalized(jnp.arange(columns, dtype=jnp.int32).astype(jnp.float32), columns)[None, :]
    filtered_list = []
    weight_sum = jnp.zeros((TILES,), jnp.float32)
    for epoch_index in range(EPOCHS):
        per_row = jnp.repeat(coeffs[epoch_index], H, axis=0)
        model = jnp.zeros((rows, columns), jnp.float32)
        for basis_index in range(NB):
            spatial = per_row[:, basis_index, 0:1] + per_row[:, basis_index, 1:2] * col_pos + per_row[:, basis_index, 2:3] * row_pos
            model = model + spatial * basis_maps[basis_index]
        difference = visits[epoch_index] - model
        smoothed = conv_cols(conv_rows(jnp.pad(difference, ((F, F), (0, 0))), psf_taps[epoch_index], F), psf_taps[epoch_index], F)
        filtered_list.append((smoothed * inv_var[epoch_index]).astype(jnp.bfloat16))
        psf_power = jnp.sum(psf_taps[epoch_index] * psf_taps[epoch_index])
        weight_sum = weight_sum + psf_power * psf_power * lax.optimization_barrier(jnp.mean(inv_var[epoch_index].reshape(TILES, H, columns), axis=(1, 2)))
    scale_norm = jnp.sqrt(weight_sum)
    padded = jnp.pad(jnp.stack(filtered_list), ((0, 0), (SMAX, SMAX), (SMAX, SMAX)))

    def tile_search(tile_index):

        def visit_velocity(vel_index, best_map):
            total = jnp.zeros((H, columns), jnp.float32)
            for epoch_index in range(EPOCHS):
                shift_row = shifts[tile_index, vel_index, epoch_index, 0]
                shift_col = shifts[tile_index, vel_index, epoch_index, 1]
                window = lax.dynamic_slice(padded[epoch_index], (tile_index * H + SMAX + shift_row, SMAX + shift_col), (H, columns))
                total = total + window.astype(jnp.float32)
            candidate = total / scale_norm[tile_index]
            return jnp.where(vel_index < vel_count[tile_index], jnp.maximum(best_map, candidate), best_map)
        return lax.fori_loop(jnp.int32(0), jnp.int32(NV), visit_velocity, jnp.full((H, columns), -1e+30, jnp.float32))
    return lax.map(tile_search, jnp.arange(TILES, dtype=jnp.int32)).reshape(rows, columns)
```

```python
import functools

import jax
import jax.numpy as jnp
from jax import lax
from jax.experimental import pallas as pl
from jax.experimental.pallas import tpu as pltpu
from jax.sharding import PartitionSpec as P

SMAX = 16
LANES = 128
HALO = 16
EDGE = 8
MESH = pl.DeviceIdType.MESH
VMEM = pltpu.VMEM
SMEM = pltpu.SMEM

T_ROWS, T_TOP, T_BOT, V_TOP, V_BOT, C_TOP, C_BOT, F_MID, F_TOP, F_BOT, WEIGHT, F_UP, F_DOWN = range(13)
KINDS = 13


def split(value):
    high = value.astype(jnp.bfloat16)
    return high, (value - high.astype(jnp.float32)).astype(jnp.bfloat16)


def filter_kernel(
    tiles, epochs,
    visits, template, taps, coeffs, psf, inv_var,
    win, norm,
    tbuf, xhigh, xlow, amat, vhalo, cbuf, rowp, gmat, diff, filt, wbuf,
    send, recv,
):
    t = lax.axis_index("sky")
    e = lax.axis_index("epoch")
    height, width = visits.shape[1], visits.shape[2]
    band = template.shape[0]
    nb, ntaps = taps.shape[1], taps.shape[2]
    half = (ntaps - 1) // 2
    fhalf = (psf.shape[1] - 1) // 2
    has_up, has_down = t > 0, t < tiles - 1

    barrier = pltpu.get_barrier_semaphore()

    def greet(row, col):
        pl.semaphore_signal(barrier, inc=1, device_id=(row, col), device_id_type=MESH)

    for other in range(epochs):
        pl.when(e != other)(lambda other=other: greet(t, other))
        pl.when(has_up)(lambda other=other: greet(t - 1, other))
        pl.when(has_down)(lambda other=other: greet(t + 1, other))
    ups = jnp.where(has_up, epochs, 0)
    downs = jnp.where(has_down, epochs, 0)

    def move(src, dst, kind, send_at, recv_at, row, col):
        return pltpu.make_async_remote_copy(
            src_ref=src, dst_ref=dst, send_sem=send.at[kind, send_at], recv_sem=recv.at[kind, recv_at],
            device_id=(row, col), device_id_type=MESH,
        )

    own_at = pl.multiple_of(HALO + e * band, 8)
    own_rows = tbuf.at[pl.ds(own_at, band)]
    tail_at = HALO + height
    last = epochs - 1

    first = []
    for other in range(epochs):
        first.append((e != other, lambda other=other: move(
            template, own_rows, T_ROWS, other, e, t, other)))
    for other in range(epochs):
        first.append((jnp.logical_and(has_down, e == last), lambda other=other: move(
            template.at[pl.ds(band - HALO, HALO)], tbuf.at[pl.ds(0, HALO)], T_TOP, other, 0, t + 1, other)))
        first.append((jnp.logical_and(has_up, e == 0), lambda other=other: move(
            template.at[pl.ds(0, HALO)], tbuf.at[pl.ds(tail_at, HALO)], T_BOT, other, 0, t - 1, other)))
    first.append((has_down, lambda: move(
        visits.at[0, pl.ds(height - EDGE, EDGE)], vhalo.at[0], V_TOP, 0, 0, t + 1, e)))
    first.append((has_up, lambda: move(
        visits.at[0, pl.ds(0, EDGE)], vhalo.at[1], V_BOT, 0, 0, t - 1, e)))
    first.append((has_down, lambda: move(cbuf.at[0], cbuf.at[1], C_TOP, 0, 0, t + 1, e)))
    first.append((has_up, lambda: move(cbuf.at[0], cbuf.at[2], C_BOT, 0, 0, t - 1, e)))

    cbuf[0] = jnp.zeros(cbuf.shape[1:], jnp.float32)
    cbuf[0, 0:nb, 0:3] = coeffs[0, 0]

    pl.semaphore_wait(barrier, epochs - 1 + ups + downs)

    for cond, make in first:
        pl.when(cond)(lambda make=make: make().start())

    @pl.when(jnp.logical_not(has_up))
    def _():
        tbuf[0:HALO] = jnp.zeros((HALO, width), jnp.float32)
        vhalo[0] = jnp.zeros(vhalo.shape[1:], jnp.float32)
        cbuf[1] = jnp.zeros(cbuf.shape[1:], jnp.float32)

    @pl.when(jnp.logical_not(has_down))
    def _():
        tbuf[tail_at:tail_at + HALO] = jnp.zeros((HALO, width), jnp.float32)
        vhalo[1] = jnp.zeros(vhalo.shape[1:], jnp.float32)
        cbuf[2] = jnp.zeros(cbuf.shape[1:], jnp.float32)

    tbuf[pl.ds(own_at, band), :] = template[...]

    rowp[...] = jnp.zeros(rowp.shape, jnp.float32)
    rowp[0:nb, 0:ntaps] = taps[0]
    rows = rowp[0:nb, :]
    cols = taps[1]

    def combine(where):
        for term in range(3):
            mixed = cols * cbuf[where, 0:nb, term:term + 1]
            gmat[where, term, 0:ntaps, :] = lax.dot_general(
                mixed, rows, (((0,), (0,)), ((), ())),
                precision=lax.Precision.HIGHEST, preferred_element_type=jnp.float32)

    def shifted_rows(start, count):
        body = tbuf[pl.ds(start, count), :]
        zeros = jnp.zeros((count, LANES), jnp.float32)
        high, low = split(jnp.concatenate([zeros, body, zeros], axis=1))
        for tap in range(ntaps):
            begin = LANES + tap - half
            xhigh[tap, pl.ds(start, count), :] = high[:, begin:begin + width]
            xlow[tap, pl.ds(start, count), :] = low[:, begin:begin + width]

    def shift_band(at):
        def step(i, carry):
            shifted_rows(pl.multiple_of(at + i * 16, 16), 16)
            return carry
        lax.fori_loop(0, band // 16, step, 0)

    combine(0)
    shift_band(pl.multiple_of(HALO + e * band, 16))

    psf_power = jnp.float32(0.0)
    for k in range(2 * fhalf + 1):
        psf_power = psf_power + psf[0, k] * psf[0, k]
    mean = jnp.sum(inv_var[0]) / (height * width)
    wbuf[pl.ds(e, 1)] = jnp.full((1, 8, LANES), psf_power * psf_power * mean, jnp.float32)

    pl.when(has_up)(lambda: move(cbuf.at[0], cbuf.at[1], C_TOP, 0, 0, t, e).wait_recv())
    pl.when(has_down)(lambda: move(cbuf.at[0], cbuf.at[2], C_BOT, 0, 0, t, e).wait_recv())
    combine(1)
    combine(2)

    block = (height + 2 * EDGE) // 2
    depth = LANES
    starts = (0, height + 2 * HALO - depth)
    row_iota = lax.broadcasted_iota(jnp.int32, (height + 2 * EDGE, 1), 0)
    in_tile = lax.rem(row_iota + (height - EDGE), height).astype(jnp.float32)
    centre = (height - 1) / 2.0
    w_all = (in_tile - centre) / centre
    for which in range(2):
        w = w_all[which * block:(which + 1) * block]
        for tap in range(ntaps):
            def base(term):
                inner = jnp.broadcast_to(gmat[0, term, tap:tap + 1, :], (block - EDGE, LANES))
                outer = jnp.broadcast_to(gmat[1 + which, term, tap:tap + 1, :], (EDGE, LANES))
                return jnp.concatenate([outer, inner] if which == 0 else [inner, outer], axis=0)
            begin = which * block - starts[which]
            plain = pltpu.roll(base(0) + w * base(2), begin, 1, stride=1, stride_axis=0)
            slope = pltpu.roll(base(1), begin, 1, stride=1, stride_axis=0)
            high, low = split(jnp.concatenate([plain, slope], axis=0))
            amat[which, 0:2 * block, tap * depth:(tap + 1) * depth] = high
            amat[which, 2 * block:4 * block, tap * depth:(tap + 1) * depth] = low

    for other in range(epochs):
        @pl.when(e != other)
        def _(other=other):
            at = HALO + other * band
            region = tbuf.at[pl.ds(at, band)]
            move(region, region, T_ROWS, other, other, t, other).wait_recv()
            shift_band(at)
    pl.when(has_up)(lambda: move(
        template.at[pl.ds(0, HALO)], tbuf.at[pl.ds(0, HALO)], T_TOP, 0, 0, t, e).wait_recv())
    shifted_rows(0, HALO)
    pl.when(has_down)(lambda: move(
        template.at[pl.ds(0, HALO)], tbuf.at[pl.ds(tail_at, HALO)], T_BOT, 0, 0, t, e).wait_recv())
    shifted_rows(tail_at, HALO)
    pl.when(has_up)(lambda: move(vhalo.at[0], vhalo.at[0], V_TOP, 0, 0, t, e).wait_recv())
    pl.when(has_down)(lambda: move(vhalo.at[1], vhalo.at[1], V_BOT, 0, 0, t, e).wait_recv())

    chunk = 256
    middle = (width - 1) / 2.0
    for which in range(2):
        for col in range(0, width, chunk):
            here = slice(col, col + chunk)
            rhs_high = xhigh[:, starts[which]:starts[which] + depth, here].reshape(ntaps * depth, chunk)
            rhs_low = xlow[:, starts[which]:starts[which] + depth, here].reshape(ntaps * depth, chunk)
            big = jnp.dot(amat[which], rhs_high, preferred_element_type=jnp.float32)
            small = jnp.dot(amat[which, 0:2 * block], rhs_low, preferred_element_type=jnp.float32)
            both = big[0:2 * block] + (big[2 * block:4 * block] + small)
            place = (lax.broadcasted_iota(jnp.int32, (1, chunk), 1) + col).astype(jnp.float32)
            u = (place - middle) / middle
            model = both[0:block] + u * both[block:2 * block]
            if which == 0:
                outside = jnp.where(has_up, vhalo[0, :, here] - model[0:EDGE], 0.0)
                diff[0:EDGE, here] = outside
                diff[EDGE:block, here] = visits[0, 0:block - EDGE, here] - model[EDGE:]
            else:
                inside = block - EDGE
                diff[block:2 * block - EDGE, here] = visits[0, height - inside:height, here] - model[0:inside]
                outside = jnp.where(has_down, vhalo[1, :, here] - model[inside:], 0.0)
                diff[2 * block - EDGE:2 * block, here] = outside

    rows_at_once = 16
    for start in range(0, height, rows_at_once):
        total = None
        for k in range(2 * fhalf + 1):
            at = start + EDGE - fhalf + k
            term = psf[0, k] * diff[at:at + rows_at_once, :]
            total = term if total is None else total + term
        zeros = jnp.zeros((rows_at_once, LANES), jnp.float32)
        padded = jnp.concatenate([zeros, total, zeros], axis=1)
        smooth = None
        for k in range(2 * fhalf + 1):
            begin = LANES + k - fhalf
            term = psf[0, k] * padded[:, begin:begin + width]
            smooth = term if smooth is None else smooth + term
        filt[start:start + rows_at_once, :] = (
            smooth * inv_var[0, start:start + rows_at_once, :]).astype(jnp.bfloat16)

    top = pl.ds(0, SMAX)
    mid = pl.ds(SMAX, band)
    bot = pl.ds(SMAX + band, SMAX)
    second = []
    for other in range(epochs):
        away = e != other
        at = other * band
        second.append((away, lambda other=other, at=at: move(
            filt.at[pl.ds(at, band)], win.at[e, mid], F_MID, other, e, t, other)))
        if other > 0:
            second.append((away, lambda other=other, at=at: move(
                filt.at[pl.ds(at - SMAX, SMAX)], win.at[e, top], F_TOP, other, e, t, other)))
        if other < last:
            second.append((away, lambda other=other, at=at: move(
                filt.at[pl.ds(at + band, SMAX)], win.at[e, bot], F_BOT, other, e, t, other)))
        second.append((away, lambda other=other: move(
            wbuf.at[e], wbuf.at[e], WEIGHT, other, e, t, other)))
    second.append((has_down, lambda: move(
        filt.at[pl.ds(height - SMAX, SMAX)], win.at[e, top], F_UP, 0, e, t + 1, 0)))
    second.append((has_up, lambda: move(
        filt.at[pl.ds(0, SMAX)], win.at[e, bot], F_DOWN, 0, e, t - 1, last)))
    for cond, make in second:
        pl.when(cond)(lambda make=make: make().start())

    own = pl.multiple_of(e * band, 16)
    win[pl.ds(e, 1), mid, :] = filt[pl.ds(own, band), :][None]

    @pl.when(e > 0)
    def _():
        win[pl.ds(e, 1), top, :] = filt[pl.ds(pl.multiple_of(own - SMAX, 16), SMAX), :][None]

    @pl.when(e < last)
    def _():
        win[pl.ds(e, 1), bot, :] = filt[pl.ds(pl.multiple_of(own + band, 16), SMAX), :][None]

    blank = jnp.zeros((epochs, SMAX, width), jnp.bfloat16)

    @pl.when(jnp.logical_and(e == 0, jnp.logical_not(has_up)))
    def _():
        win[:, top, :] = blank

    @pl.when(jnp.logical_and(e == last, jnp.logical_not(has_down)))
    def _():
        win[:, bot, :] = blank

    small = filt.at[pl.ds(0, SMAX)]
    for other in range(epochs):
        away = e != other
        pl.when(away)(lambda other=other: move(
            filt.at[pl.ds(0, band)], win.at[other, mid], F_MID, other, other, t, other).wait_recv())
        pl.when(jnp.logical_and(away, e > 0))(lambda other=other: move(
            small, win.at[other, top], F_TOP, other, other, t, other).wait_recv())
        pl.when(jnp.logical_and(away, e < last))(lambda other=other: move(
            small, win.at[other, bot], F_BOT, other, other, t, other).wait_recv())
        pl.when(away)(lambda other=other: move(
            wbuf.at[other], wbuf.at[other], WEIGHT, other, other, t, other).wait_recv())
        pl.when(jnp.logical_and(has_up, e == 0))(lambda other=other: move(
            small, win.at[other, top], F_UP, 0, other, t, other).wait_recv())
        pl.when(jnp.logical_and(has_down, e == last))(lambda other=other: move(
            small, win.at[other, bot], F_DOWN, 0, other, t, other).wait_recv())

    norm[...] = jnp.sqrt(jnp.sum(wbuf[...], axis=0))
    for cond, make in first + second:
        pl.when(cond)(lambda make=make: make().wait_send())


def search_kernel(epochs, win, norm, shifts, count, best, wide):
    band, width = best.shape
    rows = win.shape[1]
    parts = width // LANES

    def widen(i, carry):
        at = pl.multiple_of(i * 16, 16)
        for epoch in range(epochs):
            body = win[epoch, pl.ds(at, 16), :].astype(jnp.float32)
            padded = jnp.concatenate([body, jnp.zeros((16, LANES), jnp.float32)], axis=1)
            padded = pltpu.roll(padded, SMAX, 1)
            for part in range(parts + 1):
                wide[epoch, part, pl.ds(at, 16), :] = padded[:, part * LANES:(part + 1) * LANES]
        return carry

    lax.fori_loop(0, rows // 16, widen, 0)
    step = 16
    lane = lax.broadcasted_iota(jnp.int32, (step, LANES), 1)

    def stack(vel, start):
        sums = [None] * parts
        for epoch in range(epochs):
            down = shifts[0, vel, epoch, 0] + SMAX
            right = shifts[0, vel, epoch, 1] + SMAX
            turn = lax.rem(LANES - right, LANES)
            inside = lane < LANES - right
            turned = [
                pltpu.roll(wide[epoch, part, pl.ds(start + down, step), :], turn, 1)
                for part in range(parts + 1)
            ]
            for part in range(parts):
                piece = jnp.where(inside, turned[part], turned[part + 1])
                sums[part] = piece if sums[part] is None else sums[part] + piece
        return sums

    for start in range(0, band, step):
        def visit(vel, held, start=start):
            return tuple(jnp.maximum(a, b) for a, b in zip(held, stack(vel, start)))

        held = lax.fori_loop(1, count[0], visit, tuple(stack(0, start)))
        scale = norm[0:1, 0:1]
        for part in range(parts):
            best[start:start + step, part * LANES:(part + 1) * LANES] = jnp.maximum(held[part] / scale, -1e30)


def on_device(tiles, epochs, visits, template, basis_taps, coeffs, psf_taps, inv_var, shifts, vel_count):
    height, width = visits.shape[1], visits.shape[2]
    band = template.shape[0]
    nb, ntaps = basis_taps.shape[1], basis_taps.shape[2]
    pad_nb = -(-nb // 8) * 8
    pad_taps = -(-ntaps // 8) * 8
    block = (height + 2 * EDGE) // 2
    tall = height + 2 * HALO
    vmem = pl.BlockSpec(memory_space=VMEM)
    smem = pl.BlockSpec(memory_space=SMEM)
    win, norm = pl.pallas_call(
        functools.partial(filter_kernel, tiles, epochs),
        out_shape=(
            jax.ShapeDtypeStruct((epochs, band + 2 * SMAX, width), jnp.bfloat16),
            jax.ShapeDtypeStruct((8, LANES), jnp.float32),
        ),
        in_specs=[vmem, vmem, vmem, vmem, smem, vmem],
        out_specs=(vmem, vmem),
        scratch_shapes=[
            VMEM((tall, width), jnp.float32),
            VMEM((ntaps, tall, width), jnp.bfloat16),
            VMEM((ntaps, tall, width), jnp.bfloat16),
            VMEM((2, 4 * block, ntaps * LANES), jnp.bfloat16),
            VMEM((2, EDGE, width), jnp.float32),
            VMEM((3, pad_nb, LANES), jnp.float32),
            VMEM((pad_nb, LANES), jnp.float32),
            VMEM((3, 3, pad_taps, LANES), jnp.float32),
            VMEM((height + 2 * EDGE, width), jnp.float32),
            VMEM((height, width), jnp.bfloat16),
            VMEM((epochs, 8, LANES), jnp.float32),
            pltpu.SemaphoreType.DMA((KINDS, epochs)),
            pltpu.SemaphoreType.DMA((KINDS, epochs)),
        ],
        compiler_params=pltpu.CompilerParams(
            collective_id=0, has_side_effects=True, vmem_limit_bytes=40 * 1024 * 1024),
        name="filter",
    )(visits, template, basis_taps, coeffs, psf_taps, inv_var)
    return pl.pallas_call(
        functools.partial(search_kernel, epochs),
        out_shape=jax.ShapeDtypeStruct((band, width), jnp.float32),
        in_specs=[vmem, vmem, smem, smem],
        out_specs=vmem,
        scratch_shapes=[VMEM((epochs, width // LANES + 1, band + 2 * SMAX, LANES), jnp.float32)],
        compiler_params=pltpu.CompilerParams(vmem_limit_bytes=24 * 1024 * 1024),
        name="search",
    )(win, norm, shifts, vel_count)


def solution(mesh):
    in_specs = (
        P("epoch", "sky", None),
        P(("sky", "epoch"), None),
        P(),
        P("epoch", "sky", None, None),
        P("epoch", None),
        P("epoch", "sky", None),
        P("sky", None, None, None),
        P("sky"),
    )
    body = functools.partial(on_device, mesh.shape["sky"], mesh.shape["epoch"])
    return jax.shard_map(
        body, mesh=mesh, in_specs=in_specs, out_specs=P(("sky", "epoch"), None), check_vma=False)
```

```python
import functools

import jax
import jax.numpy as jnp
from jax import lax
from jax.experimental import pallas as pl
from jax.experimental.pallas import tpu as pltpu
from jax.sharding import PartitionSpec as P

SMAX = 16
LANES = 128
HALO = 16
EDGE = 8
PSF_ROW = 8
SMALL_ROWS = 16
MESH = pl.DeviceIdType.MESH
VMEM = pltpu.VMEM
SMEM = pltpu.SMEM

VIS, VIS_UP, VIS_DOWN, INV, SMALL, SMALL_UP, SMALL_DOWN, T_TOP, T_BOT, WEIGHT, F_TOP, F_BOT = range(12)
KINDS = 12


def split(value):
    high = value.astype(jnp.bfloat16)
    return high, (value - high.astype(jnp.float32)).astype(jnp.bfloat16)


def filter_kernel(
    tiles, epochs, ntaps, ftaps,
    visits, template, row_taps, col_taps, small, inv_var,
    win, norm,
    tbuf, xhigh, xlow, amat, vis, inv, whole, sbuf, rows_v, cols_v, gmat, diff, wbuf,
    send, recv, local,
):
    t = lax.axis_index("sky")
    e = lax.axis_index("epoch")
    height, width = visits.shape[1], visits.shape[2]
    band = template.shape[0]
    half = (ntaps - 1) // 2
    fhalf = (ftaps - 1) // 2
    last = epochs - 1
    has_up, has_down = t > 0, t < tiles - 1
    has_prev = jnp.logical_or(has_up, e > 0)
    has_next = jnp.logical_or(has_down, e < last)
    prev = (jnp.where(e > 0, t, t - 1), jnp.where(e > 0, e - 1, last))
    following = (jnp.where(e < last, t, t + 1), jnp.where(e < last, e + 1, 0))

    def span(owner):
        begin = max(0, owner * band - EDGE)
        end = min(height, owner * band + band + EDGE)
        return begin, end - begin, begin - (owner * band - EDGE)

    barrier = pltpu.get_barrier_semaphore()

    def greet(row, col):
        pl.semaphore_signal(barrier, inc=1, device_id=(row, col), device_id_type=MESH)

    for other in range(epochs):
        pl.when(e != other)(lambda other=other: greet(t, other))
        pl.when(has_up)(lambda other=other: greet(t - 1, other))
        pl.when(has_down)(lambda other=other: greet(t + 1, other))

    def near(src, dst, at):
        return pltpu.make_async_copy(src, dst, local.at[at])

    mid_t = tbuf.at[pl.ds(HALO, band)]
    near_t = near(template, mid_t, 0)
    near_rows = near(row_taps, rows_v, 1)
    near_cols = near(col_taps, cols_v, 2)
    near_small = near(small, sbuf.at[0, e], 3)
    near_whole = near(inv_var.at[0], whole, 4)

    def near_vis(owner):
        begin, count, to = span(owner)
        return near(visits.at[0, pl.ds(begin, count)], vis.at[owner, pl.ds(to, count)], 5)

    near_t.start()
    near_rows.start()
    near_cols.start()
    near_small.start()
    near_whole.start()
    for owner in range(epochs):
        pl.when(e == owner)(lambda owner=owner: near_vis(owner).start())

    def move(src, dst, kind, send_at, recv_at, where):
        return pltpu.make_async_remote_copy(
            src_ref=src, dst_ref=dst, send_sem=send.at[kind, send_at], recv_sem=recv.at[kind, recv_at],
            device_id=where, device_id_type=MESH,
        )

    def move_vis(owner, source):
        begin, count, to = span(owner)
        return move(visits.at[0, pl.ds(begin, count)], vis.at[source, pl.ds(to, count)], VIS, owner, source, (t, owner))

    def move_inv(owner, source):
        return move(inv_var.at[0, pl.ds(owner * band, band)], inv.at[source], INV, owner, source, (t, owner))

    tall = band + 2 * HALO
    outs = band + 2 * EDGE
    first = [
        (has_next, lambda: move(
            template.at[pl.ds(band - HALO, HALO)], tbuf.at[pl.ds(0, HALO)], T_TOP, 0, 0, following)),
        (has_prev, lambda: move(
            template.at[pl.ds(0, HALO)], tbuf.at[pl.ds(HALO + band, HALO)], T_BOT, 0, 0, prev)),
        (has_down, lambda: move(small, sbuf.at[1, e], SMALL_UP, 0, e, (t + 1, 0))),
        (has_up, lambda: move(small, sbuf.at[2, e], SMALL_DOWN, 0, e, (t - 1, last))),
    ]
    for other in range(epochs):
        first.append((e != other, lambda other=other: move(
            small, sbuf.at[0, e], SMALL, other, e, (t, other))))
    first.append((has_down, lambda: move(
        visits.at[0, pl.ds(height - EDGE, EDGE)], vis.at[e, pl.ds(0, EDGE)], VIS_UP, 0, e, (t + 1, 0))))
    first.append((has_up, lambda: move(
        visits.at[0, pl.ds(0, EDGE)], vis.at[e, pl.ds(outs - EDGE, EDGE)], VIS_DOWN, 0, e, (t - 1, last))))
    for other in range(epochs):
        first.append((e != other, lambda other=other: move_vis(other, e)))
    for other in range(epochs):
        first.append((e != other, lambda other=other: move_inv(other, e)))

    ups = jnp.where(has_up, epochs, 0)
    downs = jnp.where(has_down, epochs, 0)
    pl.semaphore_wait(barrier, epochs - 1 + ups + downs)
    for cond, make in first:
        pl.when(cond)(lambda make=make: make().start())

    def shifted_rows(start, count):
        body = tbuf[pl.ds(start, count), :]
        zeros = jnp.zeros((count, LANES), jnp.float32)
        high, low = split(jnp.concatenate([zeros, body, zeros], axis=1))
        for tap in range(ntaps):
            begin = LANES + tap - half
            xhigh[tap, pl.ds(start, count), :] = high[:, begin:begin + width]
            xlow[tap, pl.ds(start, count), :] = low[:, begin:begin + width]

    depth = xhigh.shape[1]
    if depth > tall:
        blank = jnp.zeros((depth - tall, width), jnp.bfloat16)
        for tap in range(ntaps):
            xhigh[tap, tall:depth, :] = blank
            xlow[tap, tall:depth, :] = blank

    near_t.wait()

    def shift_step(i, carry):
        shifted_rows(pl.multiple_of(HALO + i * 16, 16), 16)
        return carry

    lax.fori_loop(0, band // 16, shift_step, 0)

    near_small.wait()
    near_whole.wait()
    own_psf = sbuf[0, pl.ds(e, 1), PSF_ROW:PSF_ROW + 1, :]
    psf_power = jnp.sum(own_psf * own_psf)
    mean = jnp.sum(whole[...]) / (height * width)
    wbuf[pl.ds(e, 1)] = jnp.full((1, 8, LANES), psf_power * psf_power * mean, jnp.float32)
    inv[pl.ds(e, 1)] = whole[pl.ds(pl.multiple_of(e * band, 8), band), :][None]
    weights = []
    for other in range(epochs):
        weights.append((e != other, lambda other=other: move(
            wbuf.at[e], wbuf.at[e], WEIGHT, other, e, (t, other))))
    for cond, make in weights:
        pl.when(cond)(lambda make=make: make().start())

    near_rows.wait()
    near_cols.wait()
    for source in range(epochs):
        pl.when(e != source)(lambda source=source: move(
            small, sbuf.at[0, source], SMALL, source, source, (t, source)).wait_recv())
    for place, kind, at_end, exists in ((1, SMALL_UP, e == 0, has_up), (2, SMALL_DOWN, e == last, has_down)):
        @pl.when(jnp.logical_not(at_end))
        def _(place=place):
            sbuf[place] = sbuf[0]

        @pl.when(jnp.logical_and(at_end, jnp.logical_not(exists)))
        def _(place=place):
            sbuf[place] = jnp.zeros(sbuf.shape[1:], jnp.float32)

        for source in range(epochs):
            pl.when(jnp.logical_and(at_end, exists))(lambda place=place, kind=kind, source=source: move(
                small, sbuf.at[place, source], kind, 0, source, (t, e)).wait_recv())
    pad_taps = cols_v.shape[0]
    mixed = [
        cols_v[...] * sbuf[place, source, term:term + 1, :]
        for source in range(epochs) for place in range(3) for term in range(3)
    ]
    gmat[...] = jnp.dot(
        jnp.concatenate(mixed, axis=0), rows_v[...],
        precision=lax.Precision.HIGHEST, preferred_element_type=jnp.float32)

    row_iota = lax.broadcasted_iota(jnp.int32, (outs, 1), 0)
    in_tile = lax.rem(row_iota + (e * band + height - EDGE), height).astype(jnp.float32)
    centre = (height - 1) / 2.0
    w = (in_tile - centre) / centre
    total_rows = epochs * 2 * outs
    for source in range(epochs):
        for tap in range(ntaps):
            def base(term):
                def one(place, count):
                    at = ((source * 3 + place) * 3 + term) * pad_taps + tap
                    return jnp.broadcast_to(gmat[at:at + 1, :], (count, LANES))
                return jnp.concatenate([one(1, EDGE), one(0, band), one(2, EDGE)], axis=0)
            plain = pltpu.roll(base(0) + w * base(2), 0, 1, stride=1, stride_axis=0)
            slope = pltpu.roll(base(1), 0, 1, stride=1, stride_axis=0)
            high, low = split(jnp.concatenate([plain, slope], axis=0))
            at = source * 2 * outs
            amat[at:at + 2 * outs, tap * depth:(tap + 1) * depth] = high
            amat[total_rows + at:total_rows + at + 2 * outs, tap * depth:(tap + 1) * depth] = low

    @pl.when(jnp.logical_not(has_prev))
    def _():
        tbuf[0:HALO] = jnp.zeros((HALO, width), jnp.float32)
        for source in range(epochs):
            vis[source, 0:EDGE] = jnp.zeros((EDGE, width), jnp.float32)

    @pl.when(jnp.logical_not(has_next))
    def _():
        tbuf[HALO + band:tall] = jnp.zeros((HALO, width), jnp.float32)
        for source in range(epochs):
            vis[source, outs - EDGE:outs] = jnp.zeros((EDGE, width), jnp.float32)

    pl.when(has_prev)(lambda: move(
        template.at[pl.ds(0, HALO)], tbuf.at[pl.ds(0, HALO)], T_TOP, 0, 0, prev).wait_recv())
    pl.when(has_next)(lambda: move(
        template.at[pl.ds(0, HALO)], tbuf.at[pl.ds(HALO + band, HALO)], T_BOT, 0, 0, following).wait_recv())
    shifted_rows(0, HALO)
    shifted_rows(HALO + band, HALO)

    chunk = 256
    middle = (width - 1) / 2.0
    for col in range(0, width, chunk):
        here = slice(col, col + chunk)
        rhs_high = xhigh[:, :, here].reshape(ntaps * depth, chunk)
        rhs_low = xlow[:, :, here].reshape(ntaps * depth, chunk)
        big = jnp.dot(amat[...], rhs_high, preferred_element_type=jnp.float32)
        low = jnp.dot(amat[0:total_rows], rhs_low, preferred_element_type=jnp.float32)
        both = big[0:total_rows] + (big[total_rows:] + low)
        place = (lax.broadcasted_iota(jnp.int32, (1, chunk), 1) + col).astype(jnp.float32)
        u = (place - middle) / middle
        for source in range(epochs):
            at = source * 2 * outs
            diff[source, :, here] = both[at:at + outs] + u * both[at + outs:at + 2 * outs]

    for owner in range(epochs):
        @pl.when(e == owner)
        def _(owner=owner):
            near_vis(owner).wait()
            for source in range(epochs):
                if source != owner:
                    move_vis(owner, source).wait_recv()
    for source in range(epochs):
        pl.when(jnp.logical_and(e == 0, has_up))(lambda source=source: move(
            visits.at[0, pl.ds(0, EDGE)], vis.at[source, pl.ds(0, EDGE)], VIS_UP, 0, source, (t, e)).wait_recv())
        pl.when(jnp.logical_and(e == last, has_down))(lambda source=source: move(
            visits.at[0, pl.ds(0, EDGE)], vis.at[source, pl.ds(outs - EDGE, EDGE)], VIS_DOWN, 0, source,
            (t, e)).wait_recv())
    for source in range(epochs):
        diff[source] = vis[source] - diff[source]

    @pl.when(jnp.logical_not(has_prev))
    def _():
        for source in range(epochs):
            diff[source, 0:EDGE] = jnp.zeros((EDGE, width), jnp.float32)

    @pl.when(jnp.logical_not(has_next))
    def _():
        for source in range(epochs):
            diff[source, outs - EDGE:outs] = jnp.zeros((EDGE, width), jnp.float32)

    step = 16
    for source in range(epochs):
        pl.when(e != source)(lambda source=source: move(
            inv_var.at[0, pl.ds(0, band)], inv.at[source], INV, source, source, (t, source)).wait_recv())
        psf = [sbuf[0, source, PSF_ROW:PSF_ROW + 1, k:k + 1] for k in range(ftaps)]
        for start in range(0, band, step):
            total = None
            for k in range(ftaps):
                at = start + EDGE - fhalf + k
                term = psf[k] * diff[source, at:at + step, :]
                total = term if total is None else total + term
            zeros = jnp.zeros((step, LANES), jnp.float32)
            padded = jnp.concatenate([zeros, total, zeros], axis=1)
            smooth = None
            for k in range(ftaps):
                begin = LANES + k - fhalf
                term = psf[k] * padded[:, begin:begin + width]
                smooth = term if smooth is None else smooth + term
            win[source, SMAX + start:SMAX + start + step, :] = (
                smooth * inv[source, start:start + step, :]).astype(jnp.bfloat16)

    second = [
        (has_next, lambda: move(
            win.at[:, pl.ds(band, SMAX)], win.at[:, pl.ds(0, SMAX)], F_TOP, 0, 0, following)),
        (has_prev, lambda: move(
            win.at[:, pl.ds(SMAX, SMAX)], win.at[:, pl.ds(SMAX + band, SMAX)], F_BOT, 0, 0, prev)),
    ]
    for cond, make in second:
        pl.when(cond)(lambda make=make: make().start())

    @pl.when(jnp.logical_not(has_prev))
    def _():
        win[:, 0:SMAX, :] = jnp.zeros((epochs, SMAX, width), jnp.bfloat16)

    @pl.when(jnp.logical_not(has_next))
    def _():
        win[:, SMAX + band:, :] = jnp.zeros((epochs, SMAX, width), jnp.bfloat16)

    for source in range(epochs):
        pl.when(e != source)(lambda source=source: move(
            wbuf.at[source], wbuf.at[source], WEIGHT, source, source, (t, source)).wait_recv())
    norm[...] = jnp.sqrt(jnp.sum(wbuf[...], axis=0))
    for cond, make in first + weights:
        pl.when(cond)(lambda make=make: make().wait_send())
    pl.when(has_prev)(lambda: move(
        win.at[:, pl.ds(0, SMAX)], win.at[:, pl.ds(0, SMAX)], F_TOP, 0, 0, prev).wait_recv())
    pl.when(has_next)(lambda: move(
        win.at[:, pl.ds(0, SMAX)], win.at[:, pl.ds(SMAX + band, SMAX)], F_BOT, 0, 0, following).wait_recv())
    for cond, make in second:
        pl.when(cond)(lambda make=make: make().wait_send())


def search_kernel(epochs, win, norm, shifts, count, best, wide):
    band, width = best.shape
    rows = win.shape[1]
    parts = width // LANES

    def widen(i, carry):
        at = pl.multiple_of(i * 16, 16)
        for epoch in range(epochs):
            body = win[epoch, pl.ds(at, 16), :].astype(jnp.float32)
            padded = jnp.concatenate([body, jnp.zeros((16, LANES), jnp.float32)], axis=1)
            padded = pltpu.roll(padded, SMAX, 1)
            for part in range(parts + 1):
                wide[epoch, part, pl.ds(at, 16), :] = padded[:, part * LANES:(part + 1) * LANES]
        return carry

    lax.fori_loop(0, rows // 16, widen, 0)
    step = 16
    lane = lax.broadcasted_iota(jnp.int32, (step, LANES), 1)

    def stack(vel, finish):
        places = []
        for epoch in range(epochs):
            right = shifts[0, vel, epoch, 1] + SMAX
            places.append((
                shifts[0, vel, epoch, 0] + SMAX, lax.rem(LANES - right, LANES), lane < LANES - right))
        for start in range(0, band, step):
            sums = [None] * parts
            for epoch in range(epochs):
                down, turn, inside = places[epoch]
                turned = [
                    pltpu.roll(wide[epoch, part, pl.ds(start + down, step), :], turn, 1)
                    for part in range(parts + 1)
                ]
                for part in range(parts):
                    piece = jnp.where(inside, turned[part], turned[part + 1])
                    sums[part] = piece if sums[part] is None else sums[part] + piece
            for part in range(parts):
                finish((slice(start, start + step), slice(part * LANES, (part + 1) * LANES)), sums[part])

    def put(at, value):
        best[at] = value

    def raise_to(at, value):
        best[at] = jnp.maximum(best[at], value)

    def visit(vel, carry):
        stack(vel, raise_to)
        return carry

    stack(0, put)
    lax.fori_loop(1, count[0], visit, 0)
    best[...] = jnp.maximum(best[...] / norm[0:1, 0:1], -1e30)


def on_device(tiles, epochs, visits, template, basis_taps, coeffs, psf_taps, inv_var, shifts, vel_count):
    height, width = visits.shape[1], visits.shape[2]
    band = template.shape[0]
    nb, ntaps = basis_taps.shape[1], basis_taps.shape[2]
    ftaps = psf_taps.shape[1]
    pad_taps = -(-ntaps // 8) * 8
    tall = band + 2 * HALO
    outs = band + 2 * EDGE
    depth = LANES
    assert tall <= depth and nb <= LANES and band >= HALO and outs - 1 + ntaps <= depth

    row_taps = jnp.pad(basis_taps[0], ((0, LANES - nb), (0, LANES - ntaps)))
    col_taps = jnp.pad(basis_taps[1].T, ((0, pad_taps - ntaps), (0, LANES - nb)))
    terms = coeffs.shape[3]
    small = jnp.concatenate([
        jnp.pad(coeffs[0, 0].T, ((0, PSF_ROW - terms), (0, LANES - nb))),
        jnp.pad(psf_taps, ((0, SMALL_ROWS - PSF_ROW - 1), (0, LANES - ftaps))),
    ], axis=0)

    vmem = pl.BlockSpec(memory_space=VMEM)
    smem = pl.BlockSpec(memory_space=SMEM)
    hbm = pl.BlockSpec(memory_space=pltpu.HBM)
    win, norm = pl.pallas_call(
        functools.partial(filter_kernel, tiles, epochs, ntaps, ftaps),
        out_shape=(
            jax.ShapeDtypeStruct((epochs, band + 2 * SMAX, width), jnp.bfloat16),
            jax.ShapeDtypeStruct((8, LANES), jnp.float32),
        ),
        in_specs=[hbm] * 6,
        out_specs=(vmem, vmem),
        scratch_shapes=[
            VMEM((tall, width), jnp.float32),
            VMEM((ntaps, depth, width), jnp.bfloat16),
            VMEM((ntaps, depth, width), jnp.bfloat16),
            VMEM((2 * epochs * 2 * outs, ntaps * depth), jnp.bfloat16),
            VMEM((epochs, outs, width), jnp.float32),
            VMEM((epochs, band, width), jnp.float32),
            VMEM((height, width), jnp.float32),
            VMEM((3, epochs, SMALL_ROWS, LANES), jnp.float32),
            VMEM((LANES, LANES), jnp.float32),
            VMEM((pad_taps, LANES), jnp.float32),
            VMEM((epochs * 9 * pad_taps, LANES), jnp.float32),
            VMEM((epochs, outs, width), jnp.float32),
            VMEM((epochs, 8, LANES), jnp.float32),
            pltpu.SemaphoreType.DMA((KINDS, epochs)),
            pltpu.SemaphoreType.DMA((KINDS, epochs)),
            pltpu.SemaphoreType.DMA((6,)),
        ],
        compiler_params=pltpu.CompilerParams(
            collective_id=0, has_side_effects=True, vmem_limit_bytes=40 * 1024 * 1024),
        name="filter",
    )(visits, template, row_taps, col_taps, small, inv_var)
    return pl.pallas_call(
        functools.partial(search_kernel, epochs),
        out_shape=jax.ShapeDtypeStruct((band, width), jnp.float32),
        in_specs=[vmem, vmem, smem, smem],
        out_specs=vmem,
        scratch_shapes=[VMEM((epochs, width // LANES + 1, band + 2 * SMAX, LANES), jnp.float32)],
        compiler_params=pltpu.CompilerParams(vmem_limit_bytes=24 * 1024 * 1024),
        name="search",
    )(win, norm, shifts, vel_count)


def solution(mesh):
    in_specs = (
        P("epoch", "sky", None),
        P(("sky", "epoch"), None),
        P(),
        P("epoch", "sky", None, None),
        P("epoch", None),
        P("epoch", "sky", None),
        P("sky", None, None, None),
        P("sky"),
    )
    body = functools.partial(on_device, mesh.shape["sky"], mesh.shape["epoch"])
    return jax.shard_map(
        body, mesh=mesh, in_specs=in_specs, out_specs=P(("sky", "epoch"), None), check_vma=False)
```

```python
import functools

import jax
import jax.numpy as jnp
from jax import lax
from jax.experimental import pallas as pl
from jax.experimental.pallas import tpu as pltpu
from jax.sharding import PartitionSpec as P

SMAX = 16
LANES = 128
HALO = 16
EDGE = 8
PSF_ROW = 8
SMALL_ROWS = 16
MESH = pl.DeviceIdType.MESH
VMEM = pltpu.VMEM
SMEM = pltpu.SMEM

VIS, VIS_UP, VIS_DOWN, INV, SMALL, SMALL_UP, SMALL_DOWN, T_TOP, T_BOT, WEIGHT, F_TOP, F_BOT = range(12)
KINDS = 12


def split(value):
    high = value.astype(jnp.bfloat16)
    return high, (value - high.astype(jnp.float32)).astype(jnp.bfloat16)


def filter_kernel(
    tiles, epochs, ntaps, ftaps,
    visits, template, taps, coeffs, psf_taps, inv_var, shifts, count,
    best,
    win, wide, tbuf, xhigh, xlow, amat, vis, inv, whole, sbuf, rows_v, cols_v, gmat, diff, wbuf, taps_v, coeffs_v, psf_v,
    send, recv, local,
):
    t = lax.axis_index("sky")
    e = lax.axis_index("epoch")
    height, width = visits.shape[1], visits.shape[2]
    band = template.shape[0]
    half = (ntaps - 1) // 2
    fhalf = (ftaps - 1) // 2
    last = epochs - 1
    has_up, has_down = t > 0, t < tiles - 1
    has_prev = jnp.logical_or(has_up, e > 0)
    has_next = jnp.logical_or(has_down, e < last)
    prev = (jnp.where(e > 0, t, t - 1), jnp.where(e > 0, e - 1, last))
    following = (jnp.where(e < last, t, t + 1), jnp.where(e < last, e + 1, 0))

    def span(owner):
        begin = max(0, owner * band - EDGE)
        end = min(height, owner * band + band + EDGE)
        return begin, end - begin, begin - (owner * band - EDGE)

    barrier = pltpu.get_barrier_semaphore()

    def greet(row, col):
        pl.semaphore_signal(barrier, inc=1, device_id=(row, col), device_id_type=MESH)

    for other in range(epochs):
        pl.when(e != other)(lambda other=other: greet(t, other))
        pl.when(has_up)(lambda other=other: greet(t - 1, other))
        pl.when(has_down)(lambda other=other: greet(t + 1, other))

    def near(src, dst, at):
        return pltpu.make_async_copy(src, dst, local.at[at])

    mid_t = tbuf.at[pl.ds(HALO, band)]
    near_t = near(template, mid_t, 0)
    near_taps = near(taps, taps_v, 1)
    near_coeffs = near(coeffs, coeffs_v, 2)
    near_psf = near(psf_taps, psf_v, 3)
    small = sbuf.at[0, e]
    near_whole = near(inv_var.at[0], whole, 4)

    def near_vis(owner):
        begin, count, to = span(owner)
        return near(visits.at[0, pl.ds(begin, count)], vis.at[owner, pl.ds(to, count)], 5)

    near_coeffs.start()
    near_psf.start()
    near_taps.start()
    near_t.start()
    near_whole.start()
    for owner in range(epochs):
        pl.when(e == owner)(lambda owner=owner: near_vis(owner).start())

    def move(src, dst, kind, send_at, recv_at, where):
        return pltpu.make_async_remote_copy(
            src_ref=src, dst_ref=dst, send_sem=send.at[kind, send_at], recv_sem=recv.at[kind, recv_at],
            device_id=where, device_id_type=MESH,
        )

    def move_vis(owner, source):
        begin, count, to = span(owner)
        return move(visits.at[0, pl.ds(begin, count)], vis.at[source, pl.ds(to, count)], VIS, owner, source, (t, owner))

    def move_inv(owner, source):
        return move(inv_var.at[0, pl.ds(owner * band, band)], inv.at[source], INV, owner, source, (t, owner))

    tall = band + 2 * HALO
    outs = band + 2 * EDGE
    first = [
        (has_next, lambda: move(
            template.at[pl.ds(band - HALO, HALO)], tbuf.at[pl.ds(0, HALO)], T_TOP, 0, 0, following)),
        (has_prev, lambda: move(
            template.at[pl.ds(0, HALO)], tbuf.at[pl.ds(HALO + band, HALO)], T_BOT, 0, 0, prev)),
        (has_down, lambda: move(small, sbuf.at[1, e], SMALL_UP, 0, e, (t + 1, 0))),
        (has_up, lambda: move(small, sbuf.at[2, e], SMALL_DOWN, 0, e, (t - 1, last))),
    ]
    for other in range(epochs):
        first.append((e != other, lambda other=other: move(
            small, sbuf.at[0, e], SMALL, other, e, (t, other))))
    first.append((has_down, lambda: move(
        visits.at[0, pl.ds(height - EDGE, EDGE)], vis.at[e, pl.ds(0, EDGE)], VIS_UP, 0, e, (t + 1, 0))))
    first.append((has_up, lambda: move(
        visits.at[0, pl.ds(0, EDGE)], vis.at[e, pl.ds(outs - EDGE, EDGE)], VIS_DOWN, 0, e, (t - 1, last))))
    for other in range(epochs):
        first.append((e != other, lambda other=other: move_vis(other, e)))
    for other in range(epochs):
        first.append((e != other, lambda other=other: move_inv(other, e)))

    sbuf[0, pl.ds(e, 1)] = jnp.zeros((1, SMALL_ROWS, LANES), jnp.float32)
    rows_v[...] = jnp.zeros(rows_v.shape, jnp.float32)
    cols_v[...] = jnp.zeros(cols_v.shape, jnp.float32)
    near_coeffs.wait()
    near_psf.wait()
    nb = taps.shape[2]
    for term in range(coeffs.shape[0]):
        sbuf[0, pl.ds(e, 1), term:term + 1, 0:nb] = coeffs_v[term][None]
    sbuf[0, pl.ds(e, 1), PSF_ROW:PSF_ROW + 1, 0:ftaps] = psf_v[...][None]

    ups = jnp.where(has_up, epochs, 0)
    downs = jnp.where(has_down, epochs, 0)
    pl.semaphore_wait(barrier, epochs - 1 + ups + downs)
    for cond, make in first:
        pl.when(cond)(lambda make=make: make().start())

    def shifted_rows(start, count):
        body = tbuf[pl.ds(start, count), :]
        zeros = jnp.zeros((count, LANES), jnp.float32)
        high, low = split(jnp.concatenate([zeros, body, zeros], axis=1))
        for tap in range(ntaps):
            begin = LANES + tap - half
            xhigh[tap, pl.ds(start, count), :] = high[:, begin:begin + width]
            xlow[tap, pl.ds(start, count), :] = low[:, begin:begin + width]

    depth = xhigh.shape[1]
    if depth > tall:
        blank = jnp.zeros((depth - tall, width), jnp.bfloat16)
        for tap in range(ntaps):
            xhigh[tap, tall:depth, :] = blank
            xlow[tap, tall:depth, :] = blank

    near_taps.wait()
    for tap in range(ntaps):
        rows_v[tap:tap + 1, 0:nb] = taps_v[tap, 0:1, :]
        cols_v[tap:tap + 1, 0:nb] = taps_v[tap, 1:2, :]
    near_t.wait()

    def shift_step(i, carry):
        shifted_rows(pl.multiple_of(HALO + i * 16, 16), 16)
        return carry

    lax.fori_loop(0, band // 16, shift_step, 0)

    near_whole.wait()
    own_psf = sbuf[0, pl.ds(e, 1), PSF_ROW:PSF_ROW + 1, :]
    psf_power = jnp.sum(own_psf * own_psf)
    mean = jnp.sum(whole[...]) / (height * width)
    wbuf[pl.ds(e, 1)] = jnp.full((1, 8, LANES), psf_power * psf_power * mean, jnp.float32)
    inv[pl.ds(e, 1)] = whole[pl.ds(pl.multiple_of(e * band, 8), band), :][None]
    weights = []
    for other in range(epochs):
        weights.append((e != other, lambda other=other: move(
            wbuf.at[e], wbuf.at[e], WEIGHT, other, e, (t, other))))
    for cond, make in weights:
        pl.when(cond)(lambda make=make: make().start())

    for source in range(epochs):
        pl.when(e != source)(lambda source=source: move(
            small, sbuf.at[0, source], SMALL, source, source, (t, source)).wait_recv())
    for place, kind, at_end, exists in ((1, SMALL_UP, e == 0, has_up), (2, SMALL_DOWN, e == last, has_down)):
        @pl.when(jnp.logical_not(at_end))
        def _(place=place):
            sbuf[place] = sbuf[0]

        @pl.when(jnp.logical_and(at_end, jnp.logical_not(exists)))
        def _(place=place):
            sbuf[place] = jnp.zeros(sbuf.shape[1:], jnp.float32)

        for source in range(epochs):
            pl.when(jnp.logical_and(at_end, exists))(lambda place=place, kind=kind, source=source: move(
                small, sbuf.at[place, source], kind, 0, source, (t, e)).wait_recv())
    pad_taps = cols_v.shape[0]
    mixed = [
        cols_v[...] * sbuf[place, source, term:term + 1, :]
        for source in range(epochs) for place in range(3) for term in range(3)
    ]
    gmat[...] = lax.dot_general(
        jnp.concatenate(mixed, axis=0), rows_v[...], (((1,), (1,)), ((), ())),
        precision=lax.Precision.HIGHEST, preferred_element_type=jnp.float32)

    row_iota = lax.broadcasted_iota(jnp.int32, (outs, 1), 0)
    in_tile = lax.rem(row_iota + (e * band + height - EDGE), height).astype(jnp.float32)
    centre = (height - 1) / 2.0
    w = (in_tile - centre) / centre
    total_rows = epochs * 2 * outs
    for source in range(epochs):
        for tap in range(ntaps):
            def base(term):
                def one(place, count):
                    at = ((source * 3 + place) * 3 + term) * pad_taps + tap
                    return jnp.broadcast_to(gmat[at:at + 1, :], (count, LANES))
                return jnp.concatenate([one(1, EDGE), one(0, band), one(2, EDGE)], axis=0)
            plain = pltpu.roll(base(0) + w * base(2), 0, 1, stride=1, stride_axis=0)
            slope = pltpu.roll(base(1), 0, 1, stride=1, stride_axis=0)
            high, low = split(jnp.concatenate([plain, slope], axis=0))
            at = source * 2 * outs
            amat[at:at + 2 * outs, tap * depth:(tap + 1) * depth] = high
            amat[total_rows + at:total_rows + at + 2 * outs, tap * depth:(tap + 1) * depth] = low

    @pl.when(jnp.logical_not(has_prev))
    def _():
        tbuf[0:HALO] = jnp.zeros((HALO, width), jnp.float32)
        for source in range(epochs):
            vis[source, 0:EDGE] = jnp.zeros((EDGE, width), jnp.float32)

    @pl.when(jnp.logical_not(has_next))
    def _():
        tbuf[HALO + band:tall] = jnp.zeros((HALO, width), jnp.float32)
        for source in range(epochs):
            vis[source, outs - EDGE:outs] = jnp.zeros((EDGE, width), jnp.float32)

    pl.when(has_prev)(lambda: move(
        template.at[pl.ds(0, HALO)], tbuf.at[pl.ds(0, HALO)], T_TOP, 0, 0, prev).wait_recv())
    pl.when(has_next)(lambda: move(
        template.at[pl.ds(0, HALO)], tbuf.at[pl.ds(HALO + band, HALO)], T_BOT, 0, 0, following).wait_recv())
    shifted_rows(0, HALO)
    shifted_rows(HALO + band, HALO)

    chunk = 256
    middle = (width - 1) / 2.0
    for col in range(0, width, chunk):
        here = slice(col, col + chunk)
        rhs_high = xhigh[:, :, here].reshape(ntaps * depth, chunk)
        rhs_low = xlow[:, :, here].reshape(ntaps * depth, chunk)
        big = jnp.dot(amat[...], rhs_high, preferred_element_type=jnp.float32)
        low = jnp.dot(amat[0:total_rows], rhs_low, preferred_element_type=jnp.float32)
        both = big[0:total_rows] + (big[total_rows:] + low)
        place = (lax.broadcasted_iota(jnp.int32, (1, chunk), 1) + col).astype(jnp.float32)
        u = (place - middle) / middle
        for source in range(epochs):
            at = source * 2 * outs
            diff[source, :, here] = both[at:at + outs] + u * both[at + outs:at + 2 * outs]

    for owner in range(epochs):
        @pl.when(e == owner)
        def _(owner=owner):
            near_vis(owner).wait()
            for source in range(epochs):
                if source != owner:
                    move_vis(owner, source).wait_recv()
    for source in range(epochs):
        pl.when(jnp.logical_and(e == 0, has_up))(lambda source=source: move(
            visits.at[0, pl.ds(0, EDGE)], vis.at[source, pl.ds(0, EDGE)], VIS_UP, 0, source, (t, e)).wait_recv())
        pl.when(jnp.logical_and(e == last, has_down))(lambda source=source: move(
            visits.at[0, pl.ds(0, EDGE)], vis.at[source, pl.ds(outs - EDGE, EDGE)], VIS_DOWN, 0, source,
            (t, e)).wait_recv())
    for source in range(epochs):
        diff[source] = vis[source] - diff[source]

    @pl.when(jnp.logical_not(has_prev))
    def _():
        for source in range(epochs):
            diff[source, 0:EDGE] = jnp.zeros((EDGE, width), jnp.float32)

    @pl.when(jnp.logical_not(has_next))
    def _():
        for source in range(epochs):
            diff[source, outs - EDGE:outs] = jnp.zeros((EDGE, width), jnp.float32)

    @pl.when(jnp.logical_not(has_prev))
    def _():
        win[:, 0:SMAX, :] = jnp.zeros((epochs, SMAX, width), jnp.bfloat16)

    @pl.when(jnp.logical_not(has_next))
    def _():
        win[:, SMAX + band:, :] = jnp.zeros((epochs, SMAX, width), jnp.bfloat16)

    step = 16
    inner = list(range(0, band, step))
    edges = sorted({inner[0], inner[-1]})
    inner = [start for start in inner if start not in edges]
    second = []
    for turn in range(epochs):
        source = lax.rem(e + turn, epochs)
        if turn:
            move(inv_var.at[0, pl.ds(0, band)], inv.at[source], INV, 0, source, (t, source)).wait_recv()
        taps_row = sbuf[0, pl.ds(source, 1), PSF_ROW:PSF_ROW + 1, :][0]
        psf = [jnp.broadcast_to(taps_row[:, k:k + 1], (8, LANES)) for k in range(ftaps)]
        psf = [jnp.tile(value, (step // 8, width // LANES)) for value in psf]

        def smooth_rows(start):
            total = None
            for k in range(ftaps):
                at = start + EDGE - fhalf + k
                term = psf[k] * diff[pl.ds(source, 1), at:at + step, :][0]
                total = term if total is None else total + term
            zeros = jnp.zeros((step, LANES), jnp.float32)
            padded = jnp.concatenate([zeros, total, zeros], axis=1)
            smooth = None
            for k in range(ftaps):
                begin = LANES + k - fhalf
                term = psf[k] * padded[:, begin:begin + width]
                smooth = term if smooth is None else smooth + term
            value = (smooth * inv[pl.ds(source, 1), start:start + step, :][0]).astype(jnp.bfloat16)
            win[pl.ds(source, 1), SMAX + start:SMAX + start + step, :] = value[None]

        for start in edges:
            smooth_rows(start)
        pair = [
            (has_next, lambda source=source: move(
                win.at[source, pl.ds(band, SMAX)], win.at[source, pl.ds(0, SMAX)],
                F_TOP, source, source, following)),
            (has_prev, lambda source=source: move(
                win.at[source, pl.ds(SMAX, SMAX)], win.at[source, pl.ds(SMAX + band, SMAX)],
                F_BOT, source, source, prev)),
        ]
        for cond, make in pair:
            pl.when(cond)(lambda make=make: make().start())
        second += pair
        for start in inner:
            smooth_rows(start)

    for source in range(epochs):
        pl.when(e != source)(lambda source=source: move(
            wbuf.at[source], wbuf.at[source], WEIGHT, source, source, (t, source)).wait_recv())
    for cond, make in first + weights:
        pl.when(cond)(lambda make=make: make().wait_send())
    for source in range(epochs):
        pl.when(has_prev)(lambda source=source: move(
            win.at[source, pl.ds(0, SMAX)], win.at[source, pl.ds(0, SMAX)], F_TOP, 0, source, prev).wait_recv())
        pl.when(has_next)(lambda source=source: move(
            win.at[source, pl.ds(0, SMAX)], win.at[source, pl.ds(SMAX + band, SMAX)],
            F_BOT, 0, source, following).wait_recv())
    search(epochs, win, jnp.sqrt(jnp.sum(wbuf[...], axis=0)), shifts, count, best, wide)
    for cond, make in second:
        pl.when(cond)(lambda make=make: make().wait_send())


def search(epochs, win, norm, shifts, count, best, wide):
    band, width = best.shape
    rows = win.shape[1]
    parts = width // LANES

    def widen(i, carry):
        at = pl.multiple_of(i * 16, 16)
        for epoch in range(epochs):
            body = win[epoch, pl.ds(at, 16), :].astype(jnp.float32)
            padded = jnp.concatenate([body, jnp.zeros((16, LANES), jnp.float32)], axis=1)
            padded = pltpu.roll(padded, SMAX, 1)
            for part in range(parts + 1):
                wide[epoch, part, pl.ds(at, 16), :] = padded[:, part * LANES:(part + 1) * LANES]
        return carry

    lax.fori_loop(0, rows // 16, widen, 0)
    step = 16
    lane = lax.broadcasted_iota(jnp.int32, (step, LANES), 1)

    listed = count[0]
    group = 4

    def places_of(vel):
        places = []
        for epoch in range(epochs):
            right = shifts[epoch, 1, vel] + SMAX
            places.append((
                shifts[epoch, 0, vel] + SMAX, lax.rem(LANES - right, LANES), lane < LANES - right))
        return places

    def stack(places, start):
        sums = [None] * parts
        for epoch in range(epochs):
            down, turn, inside = places[epoch]
            turned = [
                pltpu.roll(wide[epoch, part, pl.ds(start + down, step), :], turn, 1)
                for part in range(parts + 1)
            ]
            for part in range(parts):
                piece = jnp.where(inside, turned[part], turned[part + 1])
                sums[part] = piece if sums[part] is None else sums[part] + piece
        return sums

    best[...] = jnp.full(best.shape, -jnp.inf, jnp.float32)

    def visit(turn, carry):
        every = [places_of(jnp.maximum(jnp.minimum(turn * group + i, listed - 1), 0)) for i in range(group)]
        for start in range(0, band, step):
            top = [best[start:start + step, part * LANES:(part + 1) * LANES] for part in range(parts)]
            for places in every:
                top = [jnp.maximum(a, b) for a, b in zip(top, stack(places, start))]
            for part in range(parts):
                best[start:start + step, part * LANES:(part + 1) * LANES] = top[part]
        return carry

    lax.fori_loop(0, -(-shifts.shape[2] // group), visit, 0)
    best[...] = jnp.maximum(best[...] / norm[0:1, 0:1], -1e30)


def on_device(tiles, epochs, visits, template, basis_taps, coeffs, psf_taps, inv_var, shifts, vel_count):
    height, width = visits.shape[1], visits.shape[2]
    band = template.shape[0]
    nb, ntaps = basis_taps.shape[1], basis_taps.shape[2]
    ftaps = psf_taps.shape[1]
    pad_taps = -(-ntaps // 8) * 8
    tall = band + 2 * HALO
    outs = band + 2 * EDGE
    depth = LANES
    assert tall <= depth and nb <= LANES and band >= HALO and outs - 1 + ntaps <= depth

    taps = jnp.transpose(basis_taps, (2, 0, 1))
    terms = jnp.transpose(coeffs[0], (2, 0, 1))
    listed = jnp.transpose(shifts[0], (1, 2, 0))
    vmem = pl.BlockSpec(memory_space=VMEM)
    smem = pl.BlockSpec(memory_space=SMEM)
    hbm = pl.BlockSpec(memory_space=pltpu.HBM)
    return pl.pallas_call(
        functools.partial(filter_kernel, tiles, epochs, ntaps, ftaps),
        out_shape=jax.ShapeDtypeStruct((band, width), jnp.float32),
        in_specs=[hbm] * 6 + [smem] * 2,
        out_specs=vmem,
        scratch_shapes=[
            VMEM((epochs, band + 2 * SMAX, width), jnp.bfloat16),
            VMEM((epochs, width // LANES + 1, band + 2 * SMAX, LANES), jnp.float32),
            VMEM((tall, width), jnp.float32),
            VMEM((ntaps, depth, width), jnp.bfloat16),
            VMEM((ntaps, depth, width), jnp.bfloat16),
            VMEM((2 * epochs * 2 * outs, ntaps * depth), jnp.bfloat16),
            VMEM((epochs, outs, width), jnp.float32),
            VMEM((epochs, band, width), jnp.float32),
            VMEM((height, width), jnp.float32),
            VMEM((3, epochs, SMALL_ROWS, LANES), jnp.float32),
            VMEM((LANES, LANES), jnp.float32),
            VMEM((pad_taps, LANES), jnp.float32),
            VMEM((epochs * 9 * pad_taps, LANES), jnp.float32),
            VMEM((epochs, outs, width), jnp.float32),
            VMEM((epochs, 8, LANES), jnp.float32),
            VMEM(taps.shape, jnp.float32),
            VMEM(terms.shape, jnp.float32),
            VMEM(psf_taps.shape, jnp.float32),
            pltpu.SemaphoreType.DMA((KINDS, epochs)),
            pltpu.SemaphoreType.DMA((KINDS, epochs)),
            pltpu.SemaphoreType.DMA((6,)),
        ],
        compiler_params=pltpu.CompilerParams(
            collective_id=0, has_side_effects=True, vmem_limit_bytes=60 * 1024 * 1024),
        name="detect",
    )(visits, template, taps, terms, psf_taps, inv_var, listed, vel_count)


def solution(mesh):
    in_specs = (
        P("epoch", "sky", None),
        P(("sky", "epoch"), None),
        P(),
        P("epoch", "sky", None, None),
        P("epoch", None),
        P("epoch", "sky", None),
        P("sky", None, None, None),
        P("sky"),
    )
    body = functools.partial(on_device, mesh.shape["sky"], mesh.shape["epoch"])
    return jax.shard_map(
        body, mesh=mesh, in_specs=in_specs, out_specs=P(("sky", "epoch"), None), check_vma=False)
```

```python
import functools

import jax
import jax.numpy as jnp
from jax import lax
from jax.experimental import pallas as pl
from jax.experimental.pallas import tpu as pltpu
from jax.sharding import PartitionSpec as P

SMAX = 16
LANES = 128
HALO = 16
EDGE = 8
PSF_ROW = 8
SMALL_ROWS = 16
MESH = pl.DeviceIdType.MESH
VMEM = pltpu.VMEM
SMEM = pltpu.SMEM

VIS, VIS_UP, VIS_DOWN, INV, SMALL, SMALL_UP, SMALL_DOWN, T_TOP, T_BOT, WEIGHT, F_TOP, F_BOT = range(12)
KINDS = 12


def split(value):
    high = value.astype(jnp.bfloat16)
    return high, (value - high.astype(jnp.float32)).astype(jnp.bfloat16)


def filter_kernel(
    tiles, epochs, ntaps, ftaps,
    visits, template, taps, coeffs, psf_taps, inv_var, shifts, count,
    best,
    win, wide, tbuf, xhigh, xlow, amat, vis, inv, whole, sbuf, rows_v, cols_v, gmat, diff, wbuf, taps_v, coeffs_v, psf_v,
    send, recv, local,
):
    t = lax.axis_index("sky")
    e = lax.axis_index("epoch")
    height, width = visits.shape[1], visits.shape[2]
    band = template.shape[0]
    half = (ntaps - 1) // 2
    fhalf = (ftaps - 1) // 2
    last = epochs - 1
    has_up, has_down = t > 0, t < tiles - 1
    has_prev = jnp.logical_or(has_up, e > 0)
    has_next = jnp.logical_or(has_down, e < last)
    prev = (jnp.where(e > 0, t, t - 1), jnp.where(e > 0, e - 1, last))
    following = (jnp.where(e < last, t, t + 1), jnp.where(e < last, e + 1, 0))

    def span(owner):
        begin = max(0, owner * band - EDGE)
        end = min(height, owner * band + band + EDGE)
        return begin, end - begin, begin - (owner * band - EDGE)

    barrier = pltpu.get_barrier_semaphore()

    def greet(row, col):
        pl.semaphore_signal(barrier, inc=1, device_id=(row, col), device_id_type=MESH)

    for other in range(epochs):
        pl.when(e != other)(lambda other=other: greet(t, other))
        pl.when(has_up)(lambda other=other: greet(t - 1, other))
        pl.when(has_down)(lambda other=other: greet(t + 1, other))

    def near(src, dst, at):
        return pltpu.make_async_copy(src, dst, local.at[at])

    mid_t = tbuf.at[pl.ds(HALO, band)]
    near_t = near(template, mid_t, 0)
    near_taps = near(taps, taps_v, 1)
    near_coeffs = near(coeffs, coeffs_v, 2)
    near_psf = near(psf_taps, psf_v, 3)
    small = sbuf.at[0, e]
    near_whole = near(inv_var.at[0], whole, 4)

    def near_vis(owner):
        begin, count, to = span(owner)
        return near(visits.at[0, pl.ds(begin, count)], vis.at[owner, pl.ds(to, count)], 5)

    near_coeffs.start()
    near_psf.start()
    near_taps.start()
    near_t.start()
    near_whole.start()
    for owner in range(epochs):
        pl.when(e == owner)(lambda owner=owner: near_vis(owner).start())

    def move(src, dst, kind, send_at, recv_at, where):
        return pltpu.make_async_remote_copy(
            src_ref=src, dst_ref=dst, send_sem=send.at[kind, send_at], recv_sem=recv.at[kind, recv_at],
            device_id=where, device_id_type=MESH,
        )

    def move_vis(owner, source):
        begin, count, to = span(owner)
        return move(visits.at[0, pl.ds(begin, count)], vis.at[source, pl.ds(to, count)], VIS, owner, source, (t, owner))

    def move_inv(owner, source):
        return move(inv_var.at[0, pl.ds(owner * band, band)], inv.at[source], INV, owner, source, (t, owner))

    tall = band + 2 * HALO
    outs = band + 2 * EDGE
    first = [
        (has_next, lambda: move(
            template.at[pl.ds(band - HALO, HALO)], tbuf.at[pl.ds(0, HALO)], T_TOP, 0, 0, following)),
        (has_prev, lambda: move(
            template.at[pl.ds(0, HALO)], tbuf.at[pl.ds(HALO + band, HALO)], T_BOT, 0, 0, prev)),
        (has_down, lambda: move(small, sbuf.at[1, e], SMALL_UP, 0, e, (t + 1, 0))),
        (has_up, lambda: move(small, sbuf.at[2, e], SMALL_DOWN, 0, e, (t - 1, last))),
    ]
    for other in range(epochs):
        first.append((e != other, lambda other=other: move(
            small, sbuf.at[0, e], SMALL, other, e, (t, other))))
    first.append((has_down, lambda: move(
        visits.at[0, pl.ds(height - EDGE, EDGE)], vis.at[e, pl.ds(0, EDGE)], VIS_UP, 0, e, (t + 1, 0))))
    first.append((has_up, lambda: move(
        visits.at[0, pl.ds(0, EDGE)], vis.at[e, pl.ds(outs - EDGE, EDGE)], VIS_DOWN, 0, e, (t - 1, last))))
    for other in range(epochs):
        first.append((e != other, lambda other=other: move_vis(other, e)))
    for other in range(epochs):
        first.append((e != other, lambda other=other: move_inv(other, e)))

    sbuf[0, pl.ds(e, 1)] = jnp.zeros((1, SMALL_ROWS, LANES), jnp.float32)
    rows_v[...] = jnp.zeros(rows_v.shape, jnp.float32)
    cols_v[...] = jnp.zeros(cols_v.shape, jnp.float32)
    near_coeffs.wait()
    near_psf.wait()
    nb = taps.shape[2]
    for term in range(coeffs.shape[0]):
        sbuf[0, pl.ds(e, 1), term:term + 1, 0:nb] = coeffs_v[term][None]
    sbuf[0, pl.ds(e, 1), PSF_ROW:PSF_ROW + 1, 0:ftaps] = psf_v[...][None]

    ups = jnp.where(has_up, epochs, 0)
    downs = jnp.where(has_down, epochs, 0)
    pl.semaphore_wait(barrier, epochs - 1 + ups + downs)
    for cond, make in first:
        pl.when(cond)(lambda make=make: make().start())

    def shifted_rows(start, count):
        body = tbuf[pl.ds(start, count), :]
        zeros = jnp.zeros((count, LANES), jnp.float32)
        high, low = split(jnp.concatenate([zeros, body, zeros], axis=1))
        for tap in range(ntaps):
            begin = LANES + tap - half
            xhigh[tap, pl.ds(start, count), :] = high[:, begin:begin + width]
            xlow[tap, pl.ds(start, count), :] = low[:, begin:begin + width]

    depth = xhigh.shape[1]
    near_taps.wait()
    for tap in range(ntaps):
        rows_v[tap:tap + 1, 0:nb] = taps_v[tap, 0:1, :]
        cols_v[tap:tap + 1, 0:nb] = taps_v[tap, 1:2, :]
    near_t.wait()

    for start in range(HALO, HALO + band, 16):
        shifted_rows(start, 16)

    near_whole.wait()
    own_psf = sbuf[0, pl.ds(e, 1), PSF_ROW:PSF_ROW + 1, :]
    psf_power = jnp.sum(own_psf * own_psf)
    mean = jnp.sum(whole[...]) / (height * width)
    wbuf[pl.ds(e, 1)] = jnp.full((1, 8, LANES), psf_power * psf_power * mean, jnp.float32)
    inv[pl.ds(e, 1)] = whole[pl.ds(pl.multiple_of(e * band, 8), band), :][None]
    weights = []
    for other in range(epochs):
        weights.append((e != other, lambda other=other: move(
            wbuf.at[e], wbuf.at[e], WEIGHT, other, e, (t, other))))
    for cond, make in weights:
        pl.when(cond)(lambda make=make: make().start())

    for source in range(epochs):
        pl.when(e != source)(lambda source=source: move(
            small, sbuf.at[0, source], SMALL, source, source, (t, source)).wait_recv())
    for place, kind, at_end, exists in ((1, SMALL_UP, e == 0, has_up), (2, SMALL_DOWN, e == last, has_down)):
        @pl.when(jnp.logical_not(at_end))
        def _(place=place):
            sbuf[place] = sbuf[0]

        @pl.when(jnp.logical_and(at_end, jnp.logical_not(exists)))
        def _(place=place):
            sbuf[place] = jnp.zeros(sbuf.shape[1:], jnp.float32)

        for source in range(epochs):
            pl.when(jnp.logical_and(at_end, exists))(lambda place=place, kind=kind, source=source: move(
                small, sbuf.at[place, source], kind, 0, source, (t, e)).wait_recv())
    pad_taps = cols_v.shape[0]
    mixed = [
        cols_v[...] * sbuf[place, source, term:term + 1, :]
        for source in range(epochs) for place in range(3) for term in range(3)
    ]
    gmat[...] = lax.dot_general(
        jnp.concatenate(mixed, axis=0), rows_v[...], (((1,), (1,)), ((), ())),
        precision=lax.Precision.HIGHEST, preferred_element_type=jnp.float32)

    row_iota = lax.broadcasted_iota(jnp.int32, (outs, 1), 0)
    in_tile = lax.rem(row_iota + (e * band + height - EDGE), height).astype(jnp.float32)
    centre = (height - 1) / 2.0
    w = (in_tile - centre) / centre
    total_rows = epochs * 2 * outs
    for source in range(epochs):
        for tap in range(ntaps):
            def base(term):
                def one(place, count):
                    at = ((source * 3 + place) * 3 + term) * pad_taps + tap
                    return jnp.broadcast_to(gmat[at:at + 1, :], (count, LANES))
                return jnp.concatenate([one(1, EDGE), one(0, band), one(2, EDGE)], axis=0)
            plain = pltpu.roll(base(0) + w * base(2), 0, 1, stride=1, stride_axis=0)
            slope = pltpu.roll(base(1), 0, 1, stride=1, stride_axis=0)
            high, low = split(jnp.concatenate([plain, slope], axis=0))
            at = source * 2 * outs
            amat[at:at + 2 * outs, tap * depth:(tap + 1) * depth] = high[:, 0:depth]
            amat[total_rows + at:total_rows + at + 2 * outs, tap * depth:(tap + 1) * depth] = low[:, 0:depth]

    @pl.when(jnp.logical_not(has_prev))
    def _():
        tbuf[0:HALO] = jnp.zeros((HALO, width), jnp.float32)
        for source in range(epochs):
            vis[source, 0:EDGE] = jnp.zeros((EDGE, width), jnp.float32)

    @pl.when(jnp.logical_not(has_next))
    def _():
        tbuf[HALO + band:tall] = jnp.zeros((HALO, width), jnp.float32)
        for source in range(epochs):
            vis[source, outs - EDGE:outs] = jnp.zeros((EDGE, width), jnp.float32)

    pl.when(has_prev)(lambda: move(
        template.at[pl.ds(0, HALO)], tbuf.at[pl.ds(0, HALO)], T_TOP, 0, 0, prev).wait_recv())
    pl.when(has_next)(lambda: move(
        template.at[pl.ds(0, HALO)], tbuf.at[pl.ds(HALO + band, HALO)], T_BOT, 0, 0, following).wait_recv())
    shifted_rows(0, HALO)
    shifted_rows(HALO + band, HALO)

    chunk = 256
    middle = (width - 1) / 2.0
    for col in range(0, width, chunk):
        here = slice(col, col + chunk)
        rhs_high = xhigh[:, :, here].reshape(ntaps * depth, chunk)
        rhs_low = xlow[:, :, here].reshape(ntaps * depth, chunk)
        big = jnp.dot(amat[...], rhs_high, preferred_element_type=jnp.float32)
        low = jnp.dot(amat[0:total_rows], rhs_low, preferred_element_type=jnp.float32)
        both = big[0:total_rows] + (big[total_rows:] + low)
        place = (lax.broadcasted_iota(jnp.int32, (1, chunk), 1) + col).astype(jnp.float32)
        u = (place - middle) / middle
        for source in range(epochs):
            at = source * 2 * outs
            diff[source, :, here] = both[at:at + outs] + u * both[at + outs:at + 2 * outs]

    for owner in range(epochs):
        @pl.when(e == owner)
        def _(owner=owner):
            near_vis(owner).wait()
            for source in range(epochs):
                if source != owner:
                    move_vis(owner, source).wait_recv()
    for source in range(epochs):
        pl.when(jnp.logical_and(e == 0, has_up))(lambda source=source: move(
            visits.at[0, pl.ds(0, EDGE)], vis.at[source, pl.ds(0, EDGE)], VIS_UP, 0, source, (t, e)).wait_recv())
        pl.when(jnp.logical_and(e == last, has_down))(lambda source=source: move(
            visits.at[0, pl.ds(0, EDGE)], vis.at[source, pl.ds(outs - EDGE, EDGE)], VIS_DOWN, 0, source,
            (t, e)).wait_recv())
    for source in range(epochs):
        diff[source] = vis[source] - diff[source]

    @pl.when(jnp.logical_not(has_prev))
    def _():
        for source in range(epochs):
            diff[source, 0:EDGE] = jnp.zeros((EDGE, width), jnp.float32)

    @pl.when(jnp.logical_not(has_next))
    def _():
        for source in range(epochs):
            diff[source, outs - EDGE:outs] = jnp.zeros((EDGE, width), jnp.float32)

    @pl.when(jnp.logical_not(has_prev))
    def _():
        win[:, 0:SMAX, :] = jnp.zeros((epochs, SMAX, width), jnp.bfloat16)

    @pl.when(jnp.logical_not(has_next))
    def _():
        win[:, SMAX + band:, :] = jnp.zeros((epochs, SMAX, width), jnp.bfloat16)

    step = 16
    inner = list(range(0, band, step))
    edges = sorted({inner[0], inner[-1]})
    inner = [start for start in inner if start not in edges]
    second = []
    for turn in range(epochs):
        source = lax.rem(e + turn, epochs)
        if turn:
            move(inv_var.at[0, pl.ds(0, band)], inv.at[source], INV, 0, source, (t, source)).wait_recv()
        taps_row = sbuf[0, pl.ds(source, 1), PSF_ROW:PSF_ROW + 1, :][0]
        psf = [jnp.broadcast_to(taps_row[:, k:k + 1], (8, LANES)) for k in range(ftaps)]
        psf = [jnp.tile(value, (step // 8, width // LANES)) for value in psf]

        def smooth_rows(start):
            total = None
            for k in range(ftaps):
                at = start + EDGE - fhalf + k
                term = psf[k] * diff[pl.ds(source, 1), at:at + step, :][0]
                total = term if total is None else total + term
            zeros = jnp.zeros((step, LANES), jnp.float32)
            padded = jnp.concatenate([zeros, total, zeros], axis=1)
            smooth = None
            for k in range(ftaps):
                begin = LANES + k - fhalf
                term = psf[k] * padded[:, begin:begin + width]
                smooth = term if smooth is None else smooth + term
            value = (smooth * inv[pl.ds(source, 1), start:start + step, :][0]).astype(jnp.bfloat16)
            win[pl.ds(source, 1), SMAX + start:SMAX + start + step, :] = value[None]

        for start in edges:
            smooth_rows(start)
        pair = [
            (has_next, lambda source=source: move(
                win.at[source, pl.ds(band, SMAX)], win.at[source, pl.ds(0, SMAX)],
                F_TOP, source, source, following)),
            (has_prev, lambda source=source: move(
                win.at[source, pl.ds(SMAX, SMAX)], win.at[source, pl.ds(SMAX + band, SMAX)],
                F_BOT, source, source, prev)),
        ]
        for cond, make in pair:
            pl.when(cond)(lambda make=make: make().start())
        second += pair
        for start in inner:
            smooth_rows(start)

    for start in range(SMAX, SMAX + band, 16):
        widen(win, wide, start)
    for source in range(epochs):
        pl.when(e != source)(lambda source=source: move(
            wbuf.at[source], wbuf.at[source], WEIGHT, source, source, (t, source)).wait_recv())
    for cond, make in first + weights:
        pl.when(cond)(lambda make=make: make().wait_send())
    for source in range(epochs):
        pl.when(has_prev)(lambda source=source: move(
            win.at[source, pl.ds(0, SMAX)], win.at[source, pl.ds(0, SMAX)], F_TOP, 0, source, prev).wait_recv())
        pl.when(has_next)(lambda source=source: move(
            win.at[source, pl.ds(0, SMAX)], win.at[source, pl.ds(SMAX + band, SMAX)],
            F_BOT, 0, source, following).wait_recv())
    widen(win, wide, 0)
    widen(win, wide, SMAX + band)
    search(epochs, jnp.sqrt(jnp.sum(wbuf[...], axis=0)), shifts, count, best, wide)
    for cond, make in second:
        pl.when(cond)(lambda make=make: make().wait_send())


def widen(win, wide, at):
    parts = win.shape[2] // LANES
    for epoch in range(win.shape[0]):
        body = win[epoch, at:at + 16, :].astype(jnp.float32)
        padded = jnp.concatenate([body, jnp.zeros((16, LANES), jnp.float32)], axis=1)
        padded = pltpu.roll(padded, SMAX, 1)
        for part in range(parts + 1):
            wide[epoch, part, at:at + 16, :] = padded[:, part * LANES:(part + 1) * LANES]


def search(epochs, norm, shifts, count, best, wide):
    band, width = best.shape
    parts = width // LANES

    step = 16
    lane = lax.broadcasted_iota(jnp.int32, (step, LANES), 1)

    listed = count[0]
    group = 4

    def places_of(vel):
        places = []
        for epoch in range(epochs):
            right = shifts[epoch, 1, vel] + SMAX
            places.append((
                shifts[epoch, 0, vel] + SMAX, lax.rem(LANES - right, LANES), lane < LANES - right))
        return places

    def stack(places, start):
        sums = [None] * parts
        for epoch in range(epochs):
            down, turn, inside = places[epoch]
            turned = [
                pltpu.roll(wide[epoch, part, pl.ds(start + down, step), :], turn, 1)
                for part in range(parts + 1)
            ]
            for part in range(parts):
                piece = jnp.where(inside, turned[part], turned[part + 1])
                sums[part] = piece if sums[part] is None else sums[part] + piece
        return sums

    best[...] = jnp.full(best.shape, -jnp.inf, jnp.float32)

    def visit(turn, carry):
        every = [places_of(jnp.maximum(jnp.minimum(turn * group + i, listed - 1), 0)) for i in range(group)]
        for start in range(0, band, step):
            top = [best[start:start + step, part * LANES:(part + 1) * LANES] for part in range(parts)]
            for places in every:
                top = [jnp.maximum(a, b) for a, b in zip(top, stack(places, start))]
            for part in range(parts):
                best[start:start + step, part * LANES:(part + 1) * LANES] = top[part]
        return carry

    lax.fori_loop(0, -(-shifts.shape[2] // group), visit, 0)
    best[...] = jnp.maximum(best[...] / norm[0:1, 0:1], -1e30)


def on_device(tiles, epochs, visits, template, basis_taps, coeffs, psf_taps, inv_var, shifts, vel_count):
    height, width = visits.shape[1], visits.shape[2]
    band = template.shape[0]
    nb, ntaps = basis_taps.shape[1], basis_taps.shape[2]
    ftaps = psf_taps.shape[1]
    pad_taps = -(-ntaps // 8) * 8
    tall = band + 2 * HALO
    outs = band + 2 * EDGE
    depth = tall
    assert tall <= LANES and nb <= LANES and band >= HALO and outs - 1 + ntaps <= depth

    taps = jnp.transpose(basis_taps, (2, 0, 1))
    terms = jnp.transpose(coeffs[0], (2, 0, 1))
    listed = jnp.transpose(shifts[0], (1, 2, 0))
    vmem = pl.BlockSpec(memory_space=VMEM)
    smem = pl.BlockSpec(memory_space=SMEM)
    hbm = pl.BlockSpec(memory_space=pltpu.HBM)
    return pl.pallas_call(
        functools.partial(filter_kernel, tiles, epochs, ntaps, ftaps),
        out_shape=jax.ShapeDtypeStruct((band, width), jnp.float32),
        in_specs=[hbm] * 6 + [smem] * 2,
        out_specs=vmem,
        scratch_shapes=[
            VMEM((epochs, band + 2 * SMAX, width), jnp.bfloat16),
            VMEM((epochs, width // LANES + 1, band + 2 * SMAX, LANES), jnp.float32),
            VMEM((tall, width), jnp.float32),
            VMEM((ntaps, depth, width), jnp.bfloat16),
            VMEM((ntaps, depth, width), jnp.bfloat16),
            VMEM((2 * epochs * 2 * outs, ntaps * depth), jnp.bfloat16),
            VMEM((epochs, outs, width), jnp.float32),
            VMEM((epochs, band, width), jnp.float32),
            VMEM((height, width), jnp.float32),
            VMEM((3, epochs, SMALL_ROWS, LANES), jnp.float32),
            VMEM((LANES, LANES), jnp.float32),
            VMEM((pad_taps, LANES), jnp.float32),
            VMEM((epochs * 9 * pad_taps, LANES), jnp.float32),
            VMEM((epochs, outs, width), jnp.float32),
            VMEM((epochs, 8, LANES), jnp.float32),
            VMEM(taps.shape, jnp.float32),
            VMEM(terms.shape, jnp.float32),
            VMEM(psf_taps.shape, jnp.float32),
            pltpu.SemaphoreType.DMA((KINDS, epochs)),
            pltpu.SemaphoreType.DMA((KINDS, epochs)),
            pltpu.SemaphoreType.DMA((6,)),
        ],
        compiler_params=pltpu.CompilerParams(
            collective_id=0, has_side_effects=True, vmem_limit_bytes=60 * 1024 * 1024),
        name="detect",
    )(visits, template, taps, terms, psf_taps, inv_var, listed, vel_count)


def solution(mesh):
    in_specs = (
        P("epoch", "sky", None),
        P(("sky", "epoch"), None),
        P(),
        P("epoch", "sky", None, None),
        P("epoch", None),
        P("epoch", "sky", None),
        P("sky", None, None, None),
        P("sky"),
    )
    body = functools.partial(on_device, mesh.shape["sky"], mesh.shape["epoch"])
    return jax.shard_map(
        body, mesh=mesh, in_specs=in_specs, out_specs=P(("sky", "epoch"), None), check_vma=False)
```
